32 devices in a mesh: loader: 4 (over x, core), centers: 8 (over z, y).
Axes of the slice: x: 2, y: 2, z: 4, core: 2. Of those that a mesh axis runs over, the one named last changes fastest.
Arguments:
- pool: bfloat16 [32768, 256], P('loader'), may hold values from -6 to 6
- batch_index: int32 [2048], replicated, may hold values from 0 to 32767
- targets: float32 [16, 2048], replicated, may hold values from -6 to 6
- centers: bfloat16 [262144, 256], P(('loader', 'centers')), may hold values from -6 to 6
- weights: float32 [16, 262144], P(None, ('loader', 'centers')), may hold values from -1.8 to 1.8
- nys_index: int32 [2048], P(('loader', 'centers')), may hold values from 0 to 8191, as said below
- eigvecs: float32 [2048, 128], P(('loader', 'centers')), may hold values from -0.125 to 0.125
- damping: float32 [128], replicated, may hold values from 1 to 30
Outputs:
- new_weights: float32 [16, 262144], P(None, ('loader', 'centers'))
- predictions: float32 [16, 2048], replicated
The draws below stay inside these ranges and needn't reach their ends.
Inputs may be any that keep to these rules, and one draw needn't show every extreme that they name: `nys_index`: each device's block of 64 entries names distinct local rows of that device's own 8192 centers; entry k lies in [k * 128, (k + 1) * 128); the first is 0 and the last 8191.
All inputs are finite; a program needn't handle non-finite values.
Results may differ from the reference program's by a relative error of at most 0.0049.
Values may be sent and summed in bfloat16 or wider, within the bound.
A program may use at most 256 MiB of HBM per device.

```python
import math
import jax
import jax.numpy as jnp
from jax import lax

D = 256
OUT = 16
EIG_TOP = 128
C_DEV = 8192
BATCH = 2048
NYS_DEV = 64
CENTERS = 262144
POOL = 32768
NYS = 2048
N_LOADER = 4
N_CENTERS = 8


def draw_nys_index(key, part):
    blocks = NYS // NYS_DEV
    stride = C_DEV // NYS_DEV
    offsets = jax.random.randint(key, (blocks, NYS_DEV), 0, stride)
    base = jnp.arange(NYS_DEV, dtype=jnp.int32) * stride
    picked = base[None, :] + offsets
    picked = picked.at[:, 0].set(0)
    picked = picked.at[:, NYS_DEV - 1].set(C_DEV - 1)
    return picked.reshape(-1).astype(jnp.int32)


def place_ends(values, key, least, largest):
    longest = values.shape.index(max(values.shape))
    spots = []
    for shift in (0, 1):
        where = [jax.random.randint(jax.random.fold_in(key, axis), (), 0, length) for axis, length in enumerate(values.shape)]
        where[longest] = (where[longest] + shift) % values.shape[longest]
        spots.append(tuple(where))
    return values.at[spots[0]].set(least).at[spots[1]].set(largest)


def shard_levels(stream_key, shape, split, low, largest):
    level = 1.0
    for position, shards_of in split:
        steps = jax.random.uniform(jax.random.fold_in(jax.random.fold_in(stream_key, 6), position), (shards_of,), jnp.float32, low / len(split), largest / len(split))
        level = level * jnp.repeat(jnp.exp(steps), shape[position] // shards_of).reshape((-1,) + (1,) * (len(shape) - 1 - position))
    return level


def noise(key, shape, deviation, most, split=(), held_as=jnp.bfloat16):
    array = jax.random.normal(key, shape, jnp.float32) * deviation
    if len(split) > 0:
        array = shard_levels(key, shape, split, -0.22, 0.18) * array
    return jnp.clip(array, min=-most, max=most).astype(held_as)


def setup_inputs(seed: int = 0) -> dict:
    key_list = jax.random.split(jax.random.key(seed), 9)
    return {
        "pool": noise(key_list[0], (POOL, D), 1.0, 6.0, ((0, 4),)),
        "batch_index": place_ends(jax.random.randint(key_list[1], (BATCH,), 0, POOL), jax.random.fold_in(key_list[1], 1), 0, POOL - 1).astype(jnp.int32),
        "targets": noise(key_list[2], (OUT, BATCH), 1.0, 6.0, (), jnp.float32),
        "centers": noise(key_list[3], (CENTERS, D), 1.0, 6.0, ((0, 32),)),
        "weights": noise(key_list[4], (OUT, CENTERS), 0.3, 1.8, ((1, 32),), jnp.float32),
        "nys_index": draw_nys_index(jax.random.fold_in(key_list[8], 71), 0),
        "eigvecs": noise(key_list[6], (NYS, EIG_TOP), NYS ** -0.5, 0.125, ((0, 32),), jnp.float32),
        "damping": jnp.clip(jnp.exp(jax.random.uniform(key_list[7], (EIG_TOP,), jnp.float32, math.log(1.0), math.log(30.0))), 1.0, 30.0),
    }


def kernel_tile(rows, block):
    row_sq = lax.optimization_barrier(jnp.sum(rows.astype(jnp.float32) * rows.astype(jnp.float32), axis=1))
    cen_sq = lax.optimization_barrier(jnp.sum(block.astype(jnp.float32) * block.astype(jnp.float32), axis=1))
    cross = jnp.dot(rows, block.T, preferred_element_type=jnp.float32)
    dist_sq = row_sq[:, None] + cen_sq[None, :] - 2.0 * cross
    return jnp.exp(-4.0 * jnp.sqrt(dist_sq) / math.sqrt(D)).astype(jnp.bfloat16)

def reference(pool, batch_index, targets, centers, weights, nys_index, eigvecs, damping):
    shards = N_LOADER * N_CENTERS
    batch = pool[batch_index.astype(jnp.int32)]
    cen_blocks = centers.reshape(shards, C_DEV, D)
    w_blocks = jnp.transpose(weights.reshape(OUT, shards, C_DEV), (1, 0, 2))
    idx_blocks = nys_index.reshape(shards, NYS_DEV).astype(jnp.int32)
    eig_blocks = eigvecs.reshape(shards, NYS_DEV, EIG_TOP)

    def pred_step(total, pair):
        block, w_block = pair
        kern = kernel_tile(batch, block)
        w_half = w_block.astype(jnp.bfloat16)
        return (total + jnp.dot(w_half, kern.T, preferred_element_type=jnp.float32), None)
    predictions, _ = lax.scan(pred_step, jnp.zeros((OUT, BATCH), jnp.float32), (cen_blocks, w_blocks))
    resid = (predictions - targets).astype(jnp.bfloat16)

    def grad_step(total, trio):
        block, idx, eig = trio
        kern = kernel_tile(batch, block)
        grad = jnp.dot(resid, kern, preferred_element_type=jnp.float32)
        grad_nys = grad[:, idx]
        part = jnp.dot(grad_nys, eig, precision=lax.Precision.HIGHEST, preferred_element_type=jnp.float32)
        return (total + part, grad)
    coeff, grads = lax.scan(grad_step, jnp.zeros((OUT, EIG_TOP), jnp.float32), (cen_blocks, idx_blocks, eig_blocks))

    def update(w_block, grad, idx, eig):
        delta = jnp.dot(coeff * damping[None, :], eig.T, precision=lax.Precision.HIGHEST, preferred_element_type=jnp.float32)
        fresh = w_block - 2.0 * grad
        return fresh.at[:, idx].add(2.0 * delta)
    new_blocks = jax.vmap(update)(w_blocks, grads, idx_blocks, eig_blocks)
    new_weights = jnp.transpose(new_blocks, (1, 0, 2)).reshape(OUT, shards * C_DEV)
    return (new_weights, predictions)
```

```python
import functools
import math

import jax
import jax.numpy as jnp
from jax import lax
from jax.experimental import pallas as pl
from jax.experimental.pallas import tpu as pltpu
from jax.sharding import PartitionSpec as P

PIECE = 16
SUB = 512
CT = 512
GT = 1024
PT = 512
F32, BF16 = jnp.float32, jnp.bfloat16
NT = (((1,), (1,)), ((), ()))
NN = (((1,), (0,)), ((), ()))


def dot(a, b, dims=NN):
    return lax.dot_general(a, b, dims, preferred_element_type=F32)


def kernel(
    nl, nc, nch,
    lidx_ref, nys_ref, targets_ref, eig_ref, damp_ref, pool_hbm, cen_hbm, w_hbm,
    out_ref, pred_ref,
    pool, cen, w, w_half, kern, cen_b, rows2, row_sq, batch, picked, pick_in, own,
    part, rs_in, cg_in, quarter, resid, grad, co_in, co_in2, co_own,
    sem_in, s_pick, r_pick, s_bc, r_bc, s_x, r_x, s_rs, r_rs, s_cg, r_cg, s_lg, r_lg,
    s_c1, r_c1, s_c2, r_c2,
):
    L = lax.axis_index("loader")
    c = lax.axis_index("centers")
    core_peer = L + 1 - 2 * lax.rem(L, 2)
    x_peer = L + 2 - 4 * lax.div(L, 2)
    lpeer = [lax.rem(L + d, nl) for d in range(1, nl)]
    cpeer = [lax.rem(c + d, nc) for d in range(1, nc)]
    n_cen = cen.shape[0]
    chunk = nl * nc * PIECE
    qw = nc * PIECE
    n_sub = chunk // SUB
    started = []

    def send(src, dst, ss, rs, loader, centers):
        copy = pltpu.make_async_remote_copy(
            src_ref=src, dst_ref=dst, send_sem=ss, recv_sem=rs,
            device_id=(loader, centers), device_id_type=pl.DeviceIdType.MESH,
        )
        copy.start()
        started.append(copy)
        return copy

    loads = [
        pltpu.make_async_copy(pool_hbm, pool, sem_in.at[0]),
        pltpu.make_async_copy(cen_hbm, cen, sem_in.at[1]),
        pltpu.make_async_copy(w_hbm, w, sem_in.at[2]),
    ]
    for load in loads:
        load.start()

    barrier = pltpu.get_barrier_semaphore()
    for p in lpeer:
        pl.semaphore_signal(barrier, inc=1, device_id=(p, c), device_id_type=pl.DeviceIdType.MESH)
    for p in cpeer:
        pl.semaphore_signal(barrier, inc=1, device_id=(L, p), device_id_type=pl.DeviceIdType.MESH)

    loads[0].wait()
    held = pool.shape[0]
    n_pick = lidx_ref.shape[0]
    lidx = lidx_ref[...] - L * held

    def pick(t, acc):
        spot = lax.broadcasted_iota(jnp.int32, (n_pick, PT), 1) + t * PT
        hot = jnp.where(spot == lidx, 1.0, 0.0).astype(BF16)
        return acc + dot(hot, pool[pl.ds(pl.multiple_of(t * PT, PT), PT), :])

    acc = lax.fori_loop(0, held // PT, pick, jnp.zeros((n_pick, pool.shape[1]), F32))
    picked[...] = acc.astype(BF16).reshape(picked.shape)
    pl.semaphore_wait(barrier, nl - 1 + nc - 1)
    copies = [
        send(picked.at[p], pick_in.at[L], s_pick.at[d], r_pick.at[d], p, c)
        for d, p in enumerate(lpeer)
    ]
    pick_in[L] = picked[L]

    loads[1].wait()
    ones = jnp.ones((cen.shape[1], 128), BF16)

    def norms(t, carry):
        at = pl.ds(pl.multiple_of(t * CT, CT), CT)
        sq = cen[at, :].astype(F32)
        sq = sq * sq
        hi = sq.astype(BF16)
        lo = (sq - hi.astype(F32)).astype(BF16)
        cen_b[at, :] = dot(hi, ones) + dot(lo, ones)
        return carry

    lax.fori_loop(0, n_cen // CT, norms, 0)
    loads[2].wait()
    w_half[...] = w[...].astype(BF16)

    for copy in copies:
        copy.wait_recv()
    total = pick_in[0].astype(F32)
    for p in range(1, nl):
        total = total + pick_in[p].astype(F32)
    own[...] = total.astype(BF16).reshape(own.shape)
    mine = pl.ds(pl.multiple_of(c * PIECE, PIECE), PIECE)
    bc = []
    for k in range(nch):
        bc.append([
            send(own.at[k], batch.at[k, L, mine], s_bc.at[k, d], r_bc.at[k, d], L, p)
            for d, p in enumerate(cpeer)
        ])
    for k in range(nch):
        batch[k, L, mine] = own[k]

    xs = {}

    def x_send(k):
        for copy in bc[k]:
            copy.wait_recv()
        block = batch.at[k, L]
        xs[k] = [
            send(block, block, s_x.at[k, 0], r_x.at[k, 0], x_peer, c),
            send(block, block, s_x.at[k, 1], r_x.at[k, 1], core_peer, c),
        ]

    def x_forward(k):
        xs[k][0].wait_recv()
        block = batch.at[k, x_peer]
        xs[k].append(send(block, block, s_x.at[k, 2], r_x.at[k, 2], core_peer, c))

    def x_done(k):
        xs[k][1].wait_recv()
        xs[k][2].wait_recv()

    rs, cg, lg = {}, {}, {}

    def ar_start(k):
        rs[k] = [
            send(part.at[k, p], rs_in.at[k, L], s_rs.at[k, d], r_rs.at[k, d], p, c)
            for d, p in enumerate(lpeer)
        ]
        rs_in[k, L] = part[k, L]

    def ar_mid(k):
        for copy in rs[k]:
            copy.wait_recv()
        cg_in[k, c] = sum((rs_in[k, p] for p in range(1, nl)), rs_in[k, 0])
        cg[k] = [
            send(cg_in.at[k, c], cg_in.at[k, c], s_cg.at[k, d], r_cg.at[k, d], L, p)
            for d, p in enumerate(cpeer)
        ]

    def ar_fin(k):
        for copy in cg[k]:
            copy.wait_recv()
        quarter[k, L] = sum((cg_in[k, p] for p in range(1, nc)), cg_in[k, 0])
        lg[k] = [
            send(quarter.at[k, L], quarter.at[k, L], s_lg.at[k, d], r_lg.at[k, d], p, c)
            for d, p in enumerate(lpeer)
        ]

    def residual(k):
        for copy in lg[k]:
            copy.wait_recv()
        for p in range(nl):
            lo = k * chunk + p * qw
            pred_ref[:, lo:lo + qw] = quarter[k, p]
            diff = quarter[k, p] - targets_ref[:, lo:lo + qw]
            resid[:, lo:lo + qw] = diff.astype(BF16)

    scale = -4.0 / math.sqrt(cen.shape[1]) * math.log2(math.e)

    def prepare(k):
        one = jnp.ones((8, cen.shape[1]), BF16)
        rows = batch[k].reshape(chunk, cen.shape[1])
        for s in range(n_sub):
            r = rows[s * SUB:(s + 1) * SUB].astype(F32)
            rows2[s] = (-2.0 * r).astype(BF16)
            sq = r * r
            hi = sq.astype(BF16)
            lo = (sq - hi.astype(F32)).astype(BF16)
            row_sq[s] = dot(one, hi, NT) + dot(one, lo, NT)

    def compute(k, half):
        tiles = n_cen // CT // 2
        for s in range(n_sub):
            def step(t, acc):
                at = pl.ds(pl.multiple_of((t + half * tiles) * CT, CT), CT)
                cross = dot(cen[at, :], rows2[s], NT)
                side = jnp.concatenate([cen_b[at, :]] * (SUB // 128), axis=1)
                z = jnp.maximum(cross + row_sq[s, 0:1, :] + side, 1e-30)
                val = jnp.exp2((z * lax.rsqrt(z)) * scale).astype(BF16)
                kern[k * n_sub + s, at, :] = val
                return acc + dot(w_half[:, at], val)

            acc = lax.fori_loop(0, tiles, step, jnp.zeros((16, SUB), F32))
            per = max(1, SUB // qw)
            width = min(qw, SUB)
            for q in range(per):
                lo = s * SUB + q * width
                dst = (k, lo // qw, slice(None), slice(lo % qw, lo % qw + width))
                piece = acc[:, q * width:(q + 1) * width]
                part[dst] = piece if half == 0 else part[dst] + piece

    def gradient(k):
        for s in range(n_sub):
            lo = k * chunk + s * SUB

            def step(t, carry):
                at = pl.ds(pl.multiple_of(t * GT, GT), GT)
                term = dot(resid[:, lo:lo + SUB], kern[k * n_sub + s, at, :], NT)
                if lo == 0:
                    grad[:, at] = term
                else:
                    grad[:, at] = grad[:, at] + term
                return carry

            lax.fori_loop(0, n_cen // GT, step, 0)

    x_send(0)
    x_forward(0)
    x_done(0)
    if nch > 1:
        x_send(1)
    for k in range(nch):
        prepare(k)
        compute(k, 0)
        if k + 1 < nch:
            x_forward(k + 1)
        if k >= 1:
            ar_mid(k - 1)
        compute(k, 1)
        if k + 1 < nch:
            x_done(k + 1)
        if k + 2 < nch:
            x_send(k + 2)
        ar_start(k)
        if k >= 1:
            ar_fin(k - 1)
    last = nch - 1
    for k in range(min(1, last)):
        residual(k)
        gradient(k)
    ar_mid(last)
    for k in range(1, min(2, last)):
        residual(k)
        gradient(k)
    ar_fin(last)
    for k in range(2, last):
        residual(k)
        gradient(k)
    residual(last)
    gradient(last)

    n_nys = eig_ref.shape[0]
    lane = lax.broadcasted_iota(jnp.int32, (16, 128), 1)

    def coeff_step(j, acc):
        at = pl.ds(pl.multiple_of(j * 128, 128), 128)
        hit = lane == nys_ref[j] - j * 128
        g = jnp.sum(jnp.where(hit, grad[:, at], 0.0), axis=1, keepdims=True)
        return acc + g * eig_ref[pl.ds(j, 1), :]

    co_own[0] = lax.fori_loop(0, n_nys, coeff_step, jnp.zeros((16, 128), F32), unroll=8)
    c1 = [
        send(co_own.at[0], co_in.at[L], s_c1.at[d], r_c1.at[d], p, c)
        for d, p in enumerate(lpeer)
    ]
    co_in[L] = co_own[0]
    for copy in c1:
        copy.wait_recv()
    co_own[1] = sum((co_in[p] for p in range(1, nl)), co_in[0])
    c2 = [
        send(co_own.at[1], co_in2.at[c], s_c2.at[d], r_c2.at[d], L, p)
        for d, p in enumerate(cpeer)
    ]
    co_in2[c] = co_own[1]
    for copy in c2:
        copy.wait_recv()
    coeff = sum((co_in2[p] for p in range(1, nc)), co_in2[0]) * damp_ref[...]

    def final_step(j, carry):
        at = pl.ds(pl.multiple_of(j * 128, 128), 128)
        hit = lane == nys_ref[j] - j * 128
        d = jnp.sum(coeff * eig_ref[pl.ds(j, 1), :], axis=1, keepdims=True)
        out_ref[:, at] = w[:, at] - 2.0 * grad[:, at] + jnp.where(hit, 2.0 * d, 0.0)
        return carry

    lax.fori_loop(0, n_nys, final_step, 0, unroll=8)
    for copy in started:
        copy.wait_send()


def body(pool, batch_index, targets, centers, weights, nys_index, eigvecs, damping):
    nl, nc = lax.axis_size("loader"), lax.axis_size("centers")
    rows = batch_index.shape[0]
    nch = rows // (nl * nc * PIECE)
    chunk = rows // nch
    width = centers.shape[1]
    n_cen = centers.shape[0]
    qw = nc * PIECE
    index = batch_index.reshape(nch, nl, nc, PIECE)
    index = lax.dynamic_slice_in_dim(index, lax.axis_index("centers"), 1, axis=2)
    lidx = jnp.transpose(index[:, :, 0, :], (1, 0, 2)).reshape(nl * nch * PIECE, 1)
    dma = lambda *s: [pltpu.SemaphoreType.DMA(s), pltpu.SemaphoreType.DMA(s)]
    vmem = pl.BlockSpec(memory_space=pltpu.VMEM)
    hbm = pl.BlockSpec(memory_space=pl.ANY)
    fresh, predictions = pl.pallas_call(
        functools.partial(kernel, nl, nc, nch),
        out_shape=(
            jax.ShapeDtypeStruct(weights.shape, F32),
            jax.ShapeDtypeStruct(targets.shape, F32),
        ),
        in_specs=[vmem, pl.BlockSpec(memory_space=pltpu.SMEM), vmem, vmem, vmem, hbm, hbm, hbm],
        out_specs=(vmem, vmem),
        scratch_shapes=[
            pltpu.VMEM(pool.shape, BF16),
            pltpu.VMEM(centers.shape, BF16),
            pltpu.VMEM(weights.shape, F32),
            pltpu.VMEM(weights.shape, BF16),
            pltpu.VMEM((rows // SUB, n_cen, SUB), BF16),
            pltpu.VMEM((n_cen, 128), F32),
            pltpu.VMEM((chunk // SUB, SUB, width), BF16),
            pltpu.VMEM((chunk // SUB, 8, SUB), F32),
            pltpu.VMEM((nch, nl, qw, width), BF16),
            pltpu.VMEM((nl, nch * PIECE, width), BF16),
            pltpu.VMEM((nl, nch * PIECE, width), BF16),
            pltpu.VMEM((nch, PIECE, width), BF16),
            pltpu.VMEM((nch, nl, 16, qw), F32),
            pltpu.VMEM((nch, nl, 16, qw), F32),
            pltpu.VMEM((nch, nc, 16, qw), F32),
            pltpu.VMEM((nch, nl, 16, qw), F32),
            pltpu.VMEM((16, rows), BF16),
            pltpu.VMEM(weights.shape, F32),
            pltpu.VMEM((nl, 16, 128), F32),
            pltpu.VMEM((nc, 16, 128), F32),
            pltpu.VMEM((2, 16, 128), F32),
            pltpu.SemaphoreType.DMA((3,)),
            *dma(nl - 1), *dma(nch, nc - 1), *dma(nch, 3), *dma(nch, nl - 1),
            *dma(nch, nc - 1), *dma(nch, nl - 1), *dma(nl - 1), *dma(nc - 1),
        ],
        compiler_params=pltpu.CompilerParams(
            collective_id=0, has_side_effects=True, vmem_limit_bytes=62 * 1024 * 1024
        ),
    )(lidx, nys_index, targets, eigvecs, damping.reshape(1, -1), pool, centers, weights)
    return (fresh, predictions)


def solution(mesh):
    return jax.shard_map(
        body,
        mesh=mesh,
        in_specs=(
            P("loader", None),
            P(),
            P(),
            P(("loader", "centers"), None),
            P(None, ("loader", "centers")),
            P(("loader", "centers")),
            P(("loader", "centers"), None),
            P(),
        ),
        out_specs=(P(None, ("loader", "centers")), P()),
        check_vma=False,
    )
```

```python
import functools
import math

import jax
import jax.numpy as jnp
from jax import lax
from jax.experimental import pallas as pl
from jax.experimental.pallas import tpu as pltpu
from jax.sharding import PartitionSpec as P

PIECE = 16
SUB = 512
CT = 512
GT = 1024
PT = 512
F32, BF16 = jnp.float32, jnp.bfloat16
NT = (((1,), (1,)), ((), ()))
NN = (((1,), (0,)), ((), ()))


def dot(a, b, dims=NN):
    return lax.dot_general(a, b, dims, preferred_element_type=F32)


def kernel(
    nl, nc, nch,
    index_ref, nys_ref, targets_ref, eig_ref, damp_ref, pool_hbm, cen_hbm, w_hbm,
    out_ref, pred_ref,
    pool, cen, w, w_half, kern, cen_b, rows2, row_sq, batch, picked, pick_in, own,
    part, rs_in, cg_in, quarter, resid, grad, co_in, co_in2, co_own, buf_a, buf_b,
    sem_in, s_pick, r_pick, s_bc, r_bc, s_x, r_x, s_rs, r_rs, s_cg, r_cg, s_lg, r_lg,
    s_c1, r_c1, s_c2, r_c2,
):
    L = lax.axis_index("loader")
    c = lax.axis_index("centers")
    core_peer = L + 1 - 2 * lax.rem(L, 2)
    x_peer = L + 2 - 4 * lax.div(L, 2)
    lpeer = [lax.rem(L + d, nl) for d in range(1, nl)]
    cpeer = [lax.rem(c + d, nc) for d in range(1, nc)]
    n_cen = cen.shape[0]
    chunk = nl * nc * PIECE
    qw = nc * PIECE
    n_sub = chunk // SUB
    started = []

    def send(src, dst, ss, rs, loader, centers):
        copy = pltpu.make_async_remote_copy(
            src_ref=src, dst_ref=dst, send_sem=ss, recv_sem=rs,
            device_id=(loader, centers), device_id_type=pl.DeviceIdType.MESH,
        )
        copy.start()
        started.append(copy)
        return copy

    loads = [
        pltpu.make_async_copy(pool_hbm, pool, sem_in.at[0]),
        pltpu.make_async_copy(cen_hbm, cen, sem_in.at[1]),
        pltpu.make_async_copy(w_hbm, w, sem_in.at[2]),
    ]
    for load in loads:
        load.start()

    barrier = pltpu.get_barrier_semaphore()
    for p in lpeer:
        pl.semaphore_signal(barrier, inc=1, device_id=(p, c), device_id_type=pl.DeviceIdType.MESH)
    for p in cpeer:
        pl.semaphore_signal(barrier, inc=1, device_id=(L, p), device_id_type=pl.DeviceIdType.MESH)

    loads[0].wait()
    held = pool.shape[0]
    n_pick = nl * nch * PIECE
    index = index_ref[...]
    lanes = index.shape[1]
    index = pltpu.roll(index, lax.rem(lanes - c * PIECE, lanes), 1)[:, :128] - L * held
    if nch * nl < 8:
        index = jnp.concatenate([index] * (8 // (nch * nl)), axis=0)
    index = jnp.transpose(index)[:PIECE]
    order = [k * nl + p for p in range(nl) for k in range(nch)]
    lidx = jnp.concatenate([index[:, q:q + 1] for q in order], axis=0)

    def pick(t, acc):
        spot = lax.broadcasted_iota(jnp.int32, (n_pick, PT), 1) + t * PT
        hot = jnp.where(spot == lidx, 1.0, 0.0).astype(BF16)
        return acc + dot(hot, pool[pl.ds(pl.multiple_of(t * PT, PT), PT), :])

    acc = lax.fori_loop(0, held // PT, pick, jnp.zeros((n_pick, pool.shape[1]), F32), unroll=2)
    picked[...] = acc.astype(BF16).reshape(picked.shape)
    pl.semaphore_wait(barrier, nl - 1 + nc - 1)
    copies = [
        send(picked.at[p], pick_in.at[L], s_pick.at[d], r_pick.at[d], p, c)
        for d, p in enumerate(lpeer)
    ]
    pick_in[L] = picked[L]

    loads[1].wait()
    ones = jnp.ones((cen.shape[1], 128), BF16)

    def norms(t, carry):
        at = pl.ds(pl.multiple_of(t * CT, CT), CT)
        sq = cen[at, :].astype(F32)
        sq = sq * sq
        hi = sq.astype(BF16)
        lo = (sq - hi.astype(F32)).astype(BF16)
        cen_b[at, :] = dot(hi, ones) + dot(lo, ones)
        return carry

    lax.fori_loop(0, n_cen // CT, norms, 0, unroll=2)
    loads[2].wait()
    w_half[...] = w[...].astype(BF16)

    for copy in copies:
        copy.wait_recv()
    total = pick_in[0].astype(F32)
    for p in range(1, nl):
        total = total + pick_in[p].astype(F32)
    own[...] = total.astype(BF16).reshape(own.shape)
    mine = pl.ds(pl.multiple_of(c * PIECE, PIECE), PIECE)
    bc = []
    for k in range(nch):
        bc.append([
            send(own.at[k], batch.at[k, L, mine], s_bc.at[k, d], r_bc.at[k, d], L, p)
            for d, p in enumerate(cpeer)
        ])
    for k in range(nch):
        batch[k, L, mine] = own[k]

    xs = {}

    def x_send(k):
        for copy in bc[k]:
            copy.wait_recv()
        block = batch.at[k, L]
        xs[k] = [
            send(block, block, s_x.at[k, 0], r_x.at[k, 0], x_peer, c),
            send(block, block, s_x.at[k, 1], r_x.at[k, 1], core_peer, c),
        ]

    def x_forward(k):
        xs[k][0].wait_recv()
        block = batch.at[k, x_peer]
        xs[k].append(send(block, block, s_x.at[k, 2], r_x.at[k, 2], core_peer, c))

    def x_done(k):
        xs[k][1].wait_recv()
        xs[k][2].wait_recv()

    rs, cg, lg = {}, {}, {}

    def ar_start(k):
        rs[k] = [
            send(part.at[k, p], rs_in.at[k, L], s_rs.at[k, d], r_rs.at[k, d], p, c)
            for d, p in enumerate(lpeer)
        ]
        rs_in[k, L] = part[k, L]

    def ar_mid(k):
        for copy in rs[k]:
            copy.wait_recv()
        cg_in[k, c] = sum((rs_in[k, p] for p in range(1, nl)), rs_in[k, 0])
        cg[k] = [
            send(cg_in.at[k, c], cg_in.at[k, c], s_cg.at[k, d], r_cg.at[k, d], L, p)
            for d, p in enumerate(cpeer)
        ]

    def ar_fin(k):
        for copy in cg[k]:
            copy.wait_recv()
        quarter[k, L] = sum((cg_in[k, p] for p in range(1, nc)), cg_in[k, 0])
        lg[k] = [
            send(quarter.at[k, L], quarter.at[k, L], s_lg.at[k, d], r_lg.at[k, d], p, c)
            for d, p in enumerate(lpeer)
        ]

    def residual(k):
        for copy in lg[k]:
            copy.wait_recv()
        for p in range(nl):
            lo = k * chunk + p * qw
            pred_ref[:, lo:lo + qw] = quarter[k, p]
            diff = quarter[k, p] - targets_ref[:, lo:lo + qw]
            resid[:, lo:lo + qw] = diff.astype(BF16)

    scale = -4.0 / math.sqrt(cen.shape[1]) * math.log2(math.e)

    def prepare(k):
        one = jnp.ones((8, cen.shape[1]), BF16)
        rows = batch[k].reshape(chunk, cen.shape[1])
        for s in range(n_sub):
            r = rows[s * SUB:(s + 1) * SUB].astype(F32)
            rows2[s] = (-2.0 * r).astype(BF16)
            sq = r * r
            hi = sq.astype(BF16)
            lo = (sq - hi.astype(F32)).astype(BF16)
            row_sq[s] = dot(one, hi, NT) + dot(one, lo, NT)

    def cross(s, t, buf):
        at = pl.ds(pl.multiple_of(t * CT, CT), CT)
        buf[...] = dot(cen[at, :], rows2[s], NT)

    def values(k, s, t, buf):
        at = pl.ds(pl.multiple_of(t * CT, CT), CT)
        side = jnp.concatenate([cen_b[at, :]] * (SUB // 128), axis=1)
        z = jnp.maximum(buf[...] + row_sq[s, 0:1, :] + side, 1e-30)
        kern[k * n_sub + s, at, :] = jnp.exp2((z * lax.rsqrt(z)) * scale).astype(BF16)

    def weigh(k, s, t):
        at = pl.ds(pl.multiple_of(t * CT, CT), CT)
        return dot(w_half[:, at], kern[k * n_sub + s, at, :])

    tiles = n_cen // CT

    def compute(k, between):
        for s in range(n_sub):
            def step(u, acc):
                t = 2 * u
                before = weigh(k, s, jnp.maximum(t - 1, 0))
                acc = acc + jnp.where(u > 0, before, 0.0)
                cross(s, t + 1, buf_b)
                values(k, s, t, buf_a)
                cross(s, jnp.minimum(t + 2, tiles - 1), buf_a)
                acc = acc + weigh(k, s, t)
                values(k, s, t + 1, buf_b)
                return acc

            cross(s, 0, buf_a)
            acc = lax.fori_loop(0, tiles // 4, step, jnp.zeros((16, SUB), F32))
            if s == 0:
                between()
            acc = lax.fori_loop(tiles // 4, tiles // 2, step, acc)
            acc = acc + weigh(k, s, tiles - 1)
            width = min(qw, SUB)
            for q in range(SUB // width):
                lo = s * SUB + q * width
                part[k, lo // qw, :, lo % qw:lo % qw + width] = acc[:, q * width:(q + 1) * width]

    def gradient(k):
        for s in range(n_sub):
            lo = k * chunk + s * SUB

            def step(t, carry):
                at = pl.ds(pl.multiple_of(t * GT, GT), GT)
                term = dot(resid[:, lo:lo + SUB], kern[k * n_sub + s, at, :], NT)
                if lo == 0:
                    grad[:, at] = term
                else:
                    grad[:, at] = grad[:, at] + term
                return carry

            lax.fori_loop(0, n_cen // GT, step, 0, unroll=2)

    x_send(0)
    x_forward(0)
    x_done(0)
    if nch > 1:
        x_send(1)
    for k in range(nch):
        prepare(k)

        def between():
            if k + 1 < nch:
                x_forward(k + 1)
            if k >= 1:
                ar_mid(k - 1)

        compute(k, between)
        if k + 1 < nch:
            x_done(k + 1)
        if k + 2 < nch:
            x_send(k + 2)
        ar_start(k)
        if k >= 1:
            ar_fin(k - 1)
    last = nch - 1
    for k in range(min(1, last)):
        residual(k)
        gradient(k)
    ar_mid(last)
    for k in range(1, min(2, last)):
        residual(k)
        gradient(k)
    ar_fin(last)
    for k in range(2, last):
        residual(k)
        gradient(k)
    residual(last)
    gradient(last)

    n_nys = eig_ref.shape[0]
    lane = lax.broadcasted_iota(jnp.int32, (16, 128), 1)

    def coeff_step(j, acc):
        at = pl.ds(pl.multiple_of(j * 128, 128), 128)
        hit = lane == nys_ref[j] - j * 128
        g = jnp.sum(jnp.where(hit, grad[:, at], 0.0), axis=1, keepdims=True)
        return acc + g * eig_ref[pl.ds(j, 1), :]

    co_own[0] = lax.fori_loop(0, n_nys, coeff_step, jnp.zeros((16, 128), F32), unroll=8)
    c1 = [
        send(co_own.at[0], co_in.at[L], s_c1.at[d], r_c1.at[d], p, c)
        for d, p in enumerate(lpeer)
    ]
    co_in[L] = co_own[0]
    for copy in c1:
        copy.wait_recv()
    co_own[1] = sum((co_in[p] for p in range(1, nl)), co_in[0])
    c2 = [
        send(co_own.at[1], co_in2.at[c], s_c2.at[d], r_c2.at[d], L, p)
        for d, p in enumerate(cpeer)
    ]
    co_in2[c] = co_own[1]
    for copy in c2:
        copy.wait_recv()
    coeff = sum((co_in2[p] for p in range(1, nc)), co_in2[0]) * damp_ref[...]

    def final_step(j, carry):
        at = pl.ds(pl.multiple_of(j * 128, 128), 128)
        hit = lane == nys_ref[j] - j * 128
        d = jnp.sum(coeff * eig_ref[pl.ds(j, 1), :], axis=1, keepdims=True)
        out_ref[:, at] = w[:, at] - 2.0 * grad[:, at] + jnp.where(hit, 2.0 * d, 0.0)
        return carry

    lax.fori_loop(0, n_nys, final_step, 0, unroll=8)
    for copy in started:
        copy.wait_send()


def body(pool, batch_index, targets, centers, weights, nys_index, eigvecs, damping):
    nl, nc = lax.axis_size("loader"), lax.axis_size("centers")
    rows = batch_index.shape[0]
    nch = rows // (nl * nc * PIECE)
    chunk = rows // nch
    width = centers.shape[1]
    n_cen = centers.shape[0]
    qw = nc * PIECE
    index = batch_index.reshape(nch * nl, nc * PIECE)
    dma = lambda *s: [pltpu.SemaphoreType.DMA(s), pltpu.SemaphoreType.DMA(s)]
    vmem = pl.BlockSpec(memory_space=pltpu.VMEM)
    hbm = pl.BlockSpec(memory_space=pl.ANY)
    fresh, predictions = pl.pallas_call(
        functools.partial(kernel, nl, nc, nch),
        out_shape=(
            jax.ShapeDtypeStruct(weights.shape, F32),
            jax.ShapeDtypeStruct(targets.shape, F32),
        ),
        in_specs=[vmem, pl.BlockSpec(memory_space=pltpu.SMEM), vmem, vmem, vmem, hbm, hbm, hbm],
        out_specs=(vmem, vmem),
        scratch_shapes=[
            pltpu.VMEM(pool.shape, BF16),
            pltpu.VMEM(centers.shape, BF16),
            pltpu.VMEM(weights.shape, F32),
            pltpu.VMEM(weights.shape, BF16),
            pltpu.VMEM((rows // SUB, n_cen, SUB), BF16),
            pltpu.VMEM((n_cen, 128), F32),
            pltpu.VMEM((chunk // SUB, SUB, width), BF16),
            pltpu.VMEM((chunk // SUB, 8, SUB), F32),
            pltpu.VMEM((nch, nl, qw, width), BF16),
            pltpu.VMEM((nl, nch * PIECE, width), BF16),
            pltpu.VMEM((nl, nch * PIECE, width), BF16),
            pltpu.VMEM((nch, PIECE, width), BF16),
            pltpu.VMEM((nch, nl, 16, qw), F32),
            pltpu.VMEM((nch, nl, 16, qw), F32),
            pltpu.VMEM((nch, nc, 16, qw), F32),
            pltpu.VMEM((nch, nl, 16, qw), F32),
            pltpu.VMEM((16, rows), BF16),
            pltpu.VMEM(weights.shape, F32),
            pltpu.VMEM((nl, 16, 128), F32),
            pltpu.VMEM((nc, 16, 128), F32),
            pltpu.VMEM((2, 16, 128), F32),
            pltpu.VMEM((CT, SUB), F32),
            pltpu.VMEM((CT, SUB), F32),
            pltpu.SemaphoreType.DMA((3,)),
            *dma(nl - 1), *dma(nch, nc - 1), *dma(nch, 3), *dma(nch, nl - 1),
            *dma(nch, nc - 1), *dma(nch, nl - 1), *dma(nl - 1), *dma(nc - 1),
        ],
        compiler_params=pltpu.CompilerParams(
            collective_id=0, has_side_effects=True, vmem_limit_bytes=62 * 1024 * 1024
        ),
    )(index, nys_index, targets, eigvecs, damping.reshape(1, -1), pool, centers, weights)
    return (fresh, predictions)


def solution(mesh):
    return jax.shard_map(
        body,
        mesh=mesh,
        in_specs=(
            P("loader", None),
            P(),
            P(),
            P(("loader", "centers"), None),
            P(None, ("loader", "centers")),
            P(("loader", "centers")),
            P(("loader", "centers"), None),
            P(),
        ),
        out_specs=(P(None, ("loader", "centers")), P()),
        check_vma=False,
    )
```

```python
import functools
import math

import jax
import jax.numpy as jnp
from jax import lax
from jax.experimental import pallas as pl
from jax.experimental.pallas import tpu as pltpu
from jax.sharding import PartitionSpec as P

PIECE = 16
SUB = 512
CT = 512
GT = 1024
PT = 512
F32, BF16 = jnp.float32, jnp.bfloat16
NT = (((1,), (1,)), ((), ()))
NN = (((1,), (0,)), ((), ()))


def dot(a, b, dims=NN):
    return lax.dot_general(a, b, dims, preferred_element_type=F32)


def kernel(
    nl, nc, nch,
    index_ref, nys_ref, targets_ref, eig_ref, damp_ref, pool_hbm, cen_hbm, w_hbm,
    grad, pred_ref, coeff_ref,
    pool, cen, w, w_half, kern, cen_b, rows2, row_sq, batch, picked, pick_in, own,
    part, rs_in, cg_in, quarter, resid, nys_rows, nys_kern, co_in, co_in2, co_own, buf_a, buf_b,
    sem_in, s_pick, r_pick, s_bc, r_bc, s_x, r_x, s_rs, r_rs, s_cg, r_cg, s_lg, r_lg,
    s_c1, r_c1, s_c2, r_c2,
):
    L = lax.axis_index("loader")
    c = lax.axis_index("centers")
    core_peer = L + 1 - 2 * lax.rem(L, 2)
    x_peer = L + 2 - 4 * lax.div(L, 2)
    lpeer = [lax.rem(L + d, nl) for d in range(1, nl)]
    cpeer = [lax.rem(c + d, nc) for d in range(1, nc)]
    n_cen = cen.shape[0]
    chunk = nl * nc * PIECE
    qw = nc * PIECE
    n_sub = chunk // SUB
    started = []

    def send(src, dst, ss, rs, loader, centers):
        copy = pltpu.make_async_remote_copy(
            src_ref=src, dst_ref=dst, send_sem=ss, recv_sem=rs,
            device_id=(loader, centers), device_id_type=pl.DeviceIdType.MESH,
        )
        copy.start()
        started.append(copy)
        return copy

    loads = [
        pltpu.make_async_copy(pool_hbm, pool, sem_in.at[0]),
        pltpu.make_async_copy(cen_hbm, cen, sem_in.at[1]),
        pltpu.make_async_copy(w_hbm, w, sem_in.at[2]),
    ]
    for load in loads:
        load.start()

    barrier = pltpu.get_barrier_semaphore()
    for p in lpeer:
        pl.semaphore_signal(barrier, inc=1, device_id=(p, c), device_id_type=pl.DeviceIdType.MESH)
    for p in cpeer:
        pl.semaphore_signal(barrier, inc=1, device_id=(L, p), device_id_type=pl.DeviceIdType.MESH)

    loads[0].wait()
    held = pool.shape[0]
    n_pick = nl * nch * PIECE
    index = index_ref[...]
    lanes = index.shape[1]
    index = pltpu.roll(index, lax.rem(lanes - c * PIECE, lanes), 1)[:, :128] - L * held
    if nch * nl < 8:
        index = jnp.concatenate([index] * (8 // (nch * nl)), axis=0)
    index = jnp.transpose(index)[:PIECE]
    order = [k * nl + p for p in range(nl) for k in range(nch)]
    lidx = jnp.concatenate([index[:, q:q + 1] for q in order], axis=0)

    def pick(t, acc):
        spot = lax.broadcasted_iota(jnp.int32, (n_pick, PT), 1) + t * PT
        hot = jnp.where(spot == lidx, 1.0, 0.0).astype(BF16)
        return acc + dot(hot, pool[pl.ds(pl.multiple_of(t * PT, PT), PT), :])

    acc = lax.fori_loop(0, held // PT, pick, jnp.zeros((n_pick, pool.shape[1]), F32), unroll=2)
    picked[...] = acc.astype(BF16).reshape(picked.shape)
    pl.semaphore_wait(barrier, nl - 1 + nc - 1)
    copies = [
        send(picked.at[p], pick_in.at[L], s_pick.at[d], r_pick.at[d], p, c)
        for d, p in enumerate(lpeer)
    ]
    pick_in[L] = picked[L]

    loads[1].wait()
    ones = jnp.ones((cen.shape[1], 128), BF16)

    def norms(t, carry):
        at = pl.ds(pl.multiple_of(t * CT, CT), CT)
        sq = cen[at, :].astype(F32)
        sq = sq * sq
        hi = sq.astype(BF16)
        lo = (sq - hi.astype(F32)).astype(BF16)
        cen_b[at, :] = dot(hi, ones) + dot(lo, ones)
        return carry

    lax.fori_loop(0, n_cen // CT, norms, 0, unroll=2)

    n_nys = eig_ref.shape[0]
    in_block = lax.broadcasted_iota(jnp.int32, (128, cen.shape[1]), 0)

    def nystrom(j, carry):
        rows = cen[pl.ds(pl.multiple_of(j * 128, 128), 128), :].astype(F32)
        rows = jnp.where(in_block == nys_ref[j] - j * 128, rows, 0.0)
        nys_rows[pl.ds(j, 1), :] = jnp.sum(rows, axis=0, keepdims=True)
        return carry

    lax.fori_loop(0, n_nys, nystrom, 0, unroll=4)
    nys_cen = nys_rows[...].astype(BF16)
    nys_sq = jnp.sum(nys_rows[...] * nys_rows[...], axis=1, keepdims=True)
    loads[2].wait()
    w_half[...] = w[...].astype(BF16)

    for copy in copies:
        copy.wait_recv()
    total = pick_in[0].astype(F32)
    for p in range(1, nl):
        total = total + pick_in[p].astype(F32)
    own[...] = total.astype(BF16).reshape(own.shape)
    mine = pl.ds(pl.multiple_of(c * PIECE, PIECE), PIECE)
    bc = []
    for k in range(nch):
        bc.append([
            send(own.at[k], batch.at[k, L, mine], s_bc.at[k, d], r_bc.at[k, d], L, p)
            for d, p in enumerate(cpeer)
        ])
    for k in range(nch):
        batch[k, L, mine] = own[k]

    xs = {}

    def x_send(k):
        for copy in bc[k]:
            copy.wait_recv()
        block = batch.at[k, L]
        xs[k] = [
            send(block, block, s_x.at[k, 0], r_x.at[k, 0], x_peer, c),
            send(block, block, s_x.at[k, 1], r_x.at[k, 1], core_peer, c),
        ]

    def x_forward(k):
        xs[k][0].wait_recv()
        block = batch.at[k, x_peer]
        xs[k].append(send(block, block, s_x.at[k, 2], r_x.at[k, 2], core_peer, c))

    def x_done(k):
        xs[k][1].wait_recv()
        xs[k][2].wait_recv()

    rs, cg, lg = {}, {}, {}

    def ar_start(k):
        rs[k] = [
            send(part.at[k, p], rs_in.at[k, L], s_rs.at[k, d], r_rs.at[k, d], p, c)
            for d, p in enumerate(lpeer)
        ]
        rs_in[k, L] = part[k, L]

    def ar_mid(k):
        for copy in rs[k]:
            copy.wait_recv()
        cg_in[k, c] = sum((rs_in[k, p] for p in range(1, nl)), rs_in[k, 0])
        cg[k] = [
            send(cg_in.at[k, c], cg_in.at[k, c], s_cg.at[k, d], r_cg.at[k, d], L, p)
            for d, p in enumerate(cpeer)
        ]

    def ar_fin(k):
        for copy in cg[k]:
            copy.wait_recv()
        quarter[k, L] = sum((cg_in[k, p] for p in range(1, nc)), cg_in[k, 0])
        lg[k] = [
            send(quarter.at[k, L], quarter.at[k, L], s_lg.at[k, d], r_lg.at[k, d], p, c)
            for d, p in enumerate(lpeer)
        ]

    def residual(k):
        for copy in lg[k]:
            copy.wait_recv()
        for p in range(nl):
            lo = k * chunk + p * qw
            pred_ref[:, lo:lo + qw] = quarter[k, p]
            diff = quarter[k, p] - targets_ref[:, lo:lo + qw]
            resid[:, lo:lo + qw] = -2.0 * diff.astype(BF16)

    scale = -4.0 / math.sqrt(cen.shape[1])

    def prepare(k):
        one = jnp.ones((8, cen.shape[1]), BF16)
        rows = batch[k].reshape(chunk, cen.shape[1])
        for s in range(n_sub):
            r = rows[s * SUB:(s + 1) * SUB].astype(F32)
            rows2[s] = jnp.transpose((-2.0 * r).astype(BF16))
            sq = r * r
            hi = sq.astype(BF16)
            lo = (sq - hi.astype(F32)).astype(BF16)
            row_sq[s] = dot(one, hi, NT) + dot(one, lo, NT)
            z = jnp.maximum(dot(nys_cen, rows2[s]) + row_sq[s, 0:1, :] + nys_sq, 1e-30)
            nys_kern[k * n_sub + s] = jnp.exp((z * lax.rsqrt(z)) * scale).astype(BF16)

    def cross(s, t, buf):
        at = pl.ds(pl.multiple_of(t * CT, CT), CT)
        buf[...] = dot(cen[at, :], rows2[s])

    def values(k, s, t, buf):
        at = pl.ds(pl.multiple_of(t * CT, CT), CT)
        side = jnp.concatenate([cen_b[at, :]] * (SUB // 128), axis=1)
        z = jnp.maximum(buf[...] + row_sq[s, 0:1, :] + side, 1e-30)
        kern[k * n_sub + s, at, :] = jnp.exp((z * lax.rsqrt(z)) * scale).astype(BF16)

    def weigh(k, s, t):
        at = pl.ds(pl.multiple_of(t * CT, CT), CT)
        return dot(w_half[:, at], kern[k * n_sub + s, at, :])

    tiles = n_cen // CT

    def compute(k, between):
        for s in range(n_sub):
            def step(u, acc):
                t = 2 * u
                before = weigh(k, s, jnp.maximum(t - 1, 0))
                acc = acc + jnp.where(u > 0, before, 0.0)
                cross(s, t + 1, buf_b)
                values(k, s, t, buf_a)
                cross(s, jnp.minimum(t + 2, tiles - 1), buf_a)
                acc = acc + weigh(k, s, t)
                values(k, s, t + 1, buf_b)
                return acc

            cross(s, 0, buf_a)
            acc = lax.fori_loop(0, tiles // 4, step, jnp.zeros((16, SUB), F32))
            if s == 0:
                between()
            acc = lax.fori_loop(tiles // 4, tiles // 2, step, acc)
            acc = acc + weigh(k, s, tiles - 1)
            width = min(qw, SUB)
            for q in range(SUB // width):
                lo = s * SUB + q * width
                part[k, lo // qw, :, lo % qw:lo % qw + width] = acc[:, q * width:(q + 1) * width]

    gt = n_cen // GT

    def gradient(k, first=0, end=gt):
        for s in range(n_sub):
            lo = k * chunk + s * SUB

            def step(t, carry):
                at = pl.ds(pl.multiple_of(t * GT, GT), GT)
                term = dot(resid[:, lo:lo + SUB], kern[k * n_sub + s, at, :], NT)
                if lo == 0:
                    grad[:, at] = w[:, at] + term
                else:
                    grad[:, at] = grad[:, at] + term
                return carry

            lax.fori_loop(first, end, step, 0, unroll=2)

    x_send(0)
    x_forward(0)
    x_done(0)
    if nch > 1:
        x_send(1)
    for k in range(nch):
        prepare(k)

        def between():
            if k + 1 < nch:
                x_forward(k + 1)
            if k >= 1:
                ar_mid(k - 1)

        compute(k, between)
        if k + 1 < nch:
            x_done(k + 1)
        if k + 2 < nch:
            x_send(k + 2)
        ar_start(k)
        if k >= 1:
            ar_fin(k - 1)
    last = nch - 1
    for k in range(min(1, last)):
        residual(k)
        gradient(k)
    ar_mid(last)
    for k in range(1, min(2, last)):
        residual(k)
        gradient(k)
    ar_fin(last)
    for k in range(2, last):
        residual(k)
        gradient(k)
    residual(last)
    nys_grad = jnp.zeros((16, n_nys), F32)
    for q in range(nch * n_sub):
        nys_grad = nys_grad + dot(resid[:, q * SUB:(q + 1) * SUB], nys_kern[q], NT)
    co_own[0] = lax.dot_general(
        nys_grad, eig_ref[...], NN, precision=lax.Precision.HIGHEST, preferred_element_type=F32
    )
    c1 = [
        send(co_own.at[0], co_in.at[L], s_c1.at[d], r_c1.at[d], p, c)
        for d, p in enumerate(lpeer)
    ]
    co_in[L] = co_own[0]
    gradient(last, 0, gt // 2)
    for copy in c1:
        copy.wait_recv()
    co_own[1] = sum((co_in[p] for p in range(1, nl)), co_in[0])
    c2 = [
        send(co_own.at[1], co_in2.at[c], s_c2.at[d], r_c2.at[d], L, p)
        for d, p in enumerate(cpeer)
    ]
    co_in2[c] = co_own[1]
    gradient(last, gt // 2, gt)
    for copy in c2:
        copy.wait_recv()
    coeff_ref[...] = sum((co_in2[p] for p in range(1, nc)), co_in2[0]) * damp_ref[...]

    for copy in started:
        copy.wait_send()


def finish(nys_ref, eig_ref, coeff_ref, grad_ref, pred_ref, out_ref, pred_out):
    pred_out[...] = pred_ref[...]
    lane = lax.broadcasted_iota(jnp.int32, (16, 128), 1)
    delta = lax.dot_general(
        coeff_ref[...], eig_ref[...], NT, precision=lax.Precision.HIGHEST, preferred_element_type=F32
    )
    for j in range(eig_ref.shape[0]):
        lo = j * 128
        hit = lane == nys_ref[j] - lo
        out_ref[:, lo:lo + 128] = grad_ref[:, lo:lo + 128] - jnp.where(hit, delta[:, j:j + 1], 0.0)


def body(pool, batch_index, targets, centers, weights, nys_index, eigvecs, damping):
    nl, nc = lax.axis_size("loader"), lax.axis_size("centers")
    rows = batch_index.shape[0]
    nch = rows // (nl * nc * PIECE)
    chunk = rows // nch
    width = centers.shape[1]
    n_cen = centers.shape[0]
    n_nys = nys_index.shape[0]
    qw = nc * PIECE
    index = batch_index.reshape(nch * nl, nc * PIECE)
    dma = lambda *s: [pltpu.SemaphoreType.DMA(s), pltpu.SemaphoreType.DMA(s)]
    vmem = pl.BlockSpec(memory_space=pltpu.VMEM)
    hbm = pl.BlockSpec(memory_space=pl.ANY)
    smem = pl.BlockSpec(memory_space=pltpu.SMEM)
    grad, pred, coeff = pl.pallas_call(
        functools.partial(kernel, nl, nc, nch),
        out_shape=(
            jax.ShapeDtypeStruct(weights.shape, F32),
            jax.ShapeDtypeStruct(targets.shape, F32),
            jax.ShapeDtypeStruct((16, eigvecs.shape[1]), F32),
        ),
        in_specs=[vmem, smem, vmem, vmem, vmem, hbm, hbm, hbm],
        out_specs=(vmem, vmem, vmem),
        scratch_shapes=[
            pltpu.VMEM(pool.shape, BF16),
            pltpu.VMEM(centers.shape, BF16),
            pltpu.VMEM(weights.shape, F32),
            pltpu.VMEM(weights.shape, BF16),
            pltpu.VMEM((rows // SUB, n_cen, SUB), BF16),
            pltpu.VMEM((n_cen, 128), F32),
            pltpu.VMEM((chunk // SUB, width, SUB), BF16),
            pltpu.VMEM((chunk // SUB, 8, SUB), F32),
            pltpu.VMEM((nch, nl, qw, width), BF16),
            pltpu.VMEM((nl, nch * PIECE, width), BF16),
            pltpu.VMEM((nl, nch * PIECE, width), BF16),
            pltpu.VMEM((nch, PIECE, width), BF16),
            pltpu.VMEM((nch, nl, 16, qw), F32),
            pltpu.VMEM((nch, nl, 16, qw), F32),
            pltpu.VMEM((nch, nc, 16, qw), F32),
            pltpu.VMEM((nch, nl, 16, qw), F32),
            pltpu.VMEM((16, rows), BF16),
            pltpu.VMEM((n_nys, width), F32),
            pltpu.VMEM((rows // SUB, n_nys, SUB), BF16),
            pltpu.VMEM((nl, 16, 128), F32),
            pltpu.VMEM((nc, 16, 128), F32),
            pltpu.VMEM((2, 16, 128), F32),
            pltpu.VMEM((CT, SUB), F32),
            pltpu.VMEM((CT, SUB), F32),
            pltpu.SemaphoreType.DMA((3,)),
            *dma(nl - 1), *dma(nch, nc - 1), *dma(nch, 3), *dma(nch, nl - 1),
            *dma(nch, nc - 1), *dma(nch, nl - 1), *dma(nl - 1), *dma(nc - 1),
        ],
        compiler_params=pltpu.CompilerParams(
            collective_id=0, has_side_effects=True, vmem_limit_bytes=62 * 1024 * 1024
        ),
    )(index, nys_index, targets, eigvecs, damping.reshape(1, -1), pool, centers, weights)
    return pl.pallas_call(
        finish,
        out_shape=(
            jax.ShapeDtypeStruct(weights.shape, F32),
            jax.ShapeDtypeStruct(targets.shape, F32),
        ),
        in_specs=[smem, vmem, vmem, vmem, vmem],
        out_specs=(vmem, vmem),
    )(nys_index, eigvecs, coeff, grad, pred)


def solution(mesh):
    return jax.shard_map(
        body,
        mesh=mesh,
        in_specs=(
            P("loader", None),
            P(),
            P(),
            P(("loader", "centers"), None),
            P(None, ("loader", "centers")),
            P(("loader", "centers")),
            P(("loader", "centers"), None),
            P(),
        ),
        out_specs=(P(None, ("loader", "centers")), P()),
        check_vma=False,
    )
```

```python
import functools
import math

import jax
import jax.numpy as jnp
from jax import lax
from jax.experimental import pallas as pl
from jax.experimental.pallas import tpu as pltpu
from jax.sharding import PartitionSpec as P

PIECE = 16
SUB = 512
CT = 512
GT = 1024
STRIP = 16
PT = 512
F32, BF16 = jnp.float32, jnp.bfloat16
NT = (((1,), (1,)), ((), ()))
NN = (((1,), (0,)), ((), ()))


def dot(a, b, dims=NN):
    return lax.dot_general(a, b, dims, preferred_element_type=F32)


def kernel(
    nl, nc, nch,
    index_ref, nys_ref, targets_ref, eig_ref, damp_ref, pool_hbm, cen_hbm, w_hbm,
    grad, pred_ref, coeff_ref,
    pool, cen, w, w_half, kern, cen_b, rows2, row_sq, batch, picked, pick_in, own,
    part, rs_in, cg_in, quarter, resid, nys_rows, nys_kern, co_in, co_in2, co_own, buf_a, buf_b,
    sem_in, s_pick, r_pick, s_bc, r_bc, s_x, r_x, s_rs, r_rs, s_cg, r_cg, s_lg, r_lg,
    s_c1, r_c1, s_c2, r_c2,
):
    L = lax.axis_index("loader")
    c = lax.axis_index("centers")
    core_peer = L + 1 - 2 * lax.rem(L, 2)
    x_peer = L + 2 - 4 * lax.div(L, 2)
    lpeer = [lax.rem(L + d, nl) for d in range(1, nl)]
    cpeer = [lax.rem(c + d, nc) for d in range(1, nc)]
    n_cen = cen.shape[0]
    chunk = nl * nc * PIECE
    qw = nc * PIECE
    n_sub = chunk // SUB
    started = []

    def send(src, dst, ss, rs, loader, centers):
        copy = pltpu.make_async_remote_copy(
            src_ref=src, dst_ref=dst, send_sem=ss, recv_sem=rs,
            device_id=(loader, centers), device_id_type=pl.DeviceIdType.MESH,
        )
        copy.start()
        started.append(copy)
        return copy

    loads = [
        pltpu.make_async_copy(pool_hbm, pool, sem_in.at[0]),
        pltpu.make_async_copy(cen_hbm, cen, sem_in.at[1]),
        pltpu.make_async_copy(w_hbm, w, sem_in.at[2]),
    ]
    for load in loads:
        load.start()

    barrier = pltpu.get_barrier_semaphore()
    for p in lpeer:
        pl.semaphore_signal(barrier, inc=1, device_id=(p, c), device_id_type=pl.DeviceIdType.MESH)
    for p in cpeer:
        pl.semaphore_signal(barrier, inc=1, device_id=(L, p), device_id_type=pl.DeviceIdType.MESH)

    loads[0].wait()
    held = pool.shape[0]
    n_pick = nl * nch * PIECE
    index = index_ref[...]
    lanes = index.shape[1]
    index = pltpu.roll(index, lax.rem(lanes - c * PIECE, lanes), 1)[:, :128] - L * held
    if nch * nl < 8:
        index = jnp.concatenate([index] * (8 // (nch * nl)), axis=0)
    index = jnp.transpose(index)[:PIECE]
    order = [k * nl + p for p in range(nl) for k in range(nch)]
    lidx = jnp.concatenate([index[:, q:q + 1] for q in order], axis=0)

    def pick(t, acc):
        spot = lax.broadcasted_iota(jnp.int32, (n_pick, PT), 1) + t * PT
        hot = jnp.where(spot == lidx, 1.0, 0.0).astype(BF16)
        return acc + dot(hot, pool[pl.ds(pl.multiple_of(t * PT, PT), PT), :])

    acc = lax.fori_loop(0, held // PT, pick, jnp.zeros((n_pick, pool.shape[1]), F32), unroll=2)
    picked[...] = acc.astype(BF16).reshape(picked.shape)
    pl.semaphore_wait(barrier, nl - 1 + nc - 1)
    copies = [
        send(picked.at[p], pick_in.at[L], s_pick.at[d], r_pick.at[d], p, c)
        for d, p in enumerate(lpeer)
    ]
    pick_in[L] = picked[L]

    loads[1].wait()
    ones = jnp.ones((cen.shape[1], 128), BF16)

    def norms(t, carry):
        at = pl.ds(pl.multiple_of(t * 128, 128), 128)
        sq = cen[at, :].astype(F32)
        sq = sq * sq
        hi = sq.astype(BF16)
        lo = (sq - hi.astype(F32)).astype(BF16)
        cen_b[at, :] = dot(hi, ones) + dot(lo, ones)
        return carry

    lax.fori_loop(0, n_cen // 128, norms, 0, unroll=4)

    n_nys = eig_ref.shape[0]
    in_block = lax.broadcasted_iota(jnp.int32, (128, cen.shape[1]), 0)

    def nystrom(j, carry):
        rows = cen[pl.ds(pl.multiple_of(j * 128, 128), 128), :].astype(F32)
        rows = jnp.where(in_block == nys_ref[j] - j * 128, rows, 0.0)
        nys_rows[pl.ds(j, 1), :] = jnp.sum(rows, axis=0, keepdims=True)
        return carry

    lax.fori_loop(0, n_nys, nystrom, 0, unroll=4)
    nys_cen = nys_rows[...].astype(BF16)
    nys_sq = jnp.sum(nys_rows[...] * nys_rows[...], axis=1, keepdims=True)
    loads[2].wait()
    w_half[...] = w[...].astype(BF16)

    for copy in copies:
        copy.wait_recv()
    total = pick_in[0].astype(F32)
    for p in range(1, nl):
        total = total + pick_in[p].astype(F32)
    own[...] = total.astype(BF16).reshape(own.shape)
    mine = pl.ds(pl.multiple_of(c * PIECE, PIECE), PIECE)
    bc = []
    for k in range(nch):
        bc.append([
            send(own.at[k], batch.at[k, L, mine], s_bc.at[k, d], r_bc.at[k, d], L, p)
            for d, p in enumerate(cpeer)
        ])
    for k in range(nch):
        batch[k, L, mine] = own[k]

    xs = {}

    def x_send(k):
        for copy in bc[k]:
            copy.wait_recv()
        block = batch.at[k, L]
        xs[k] = [
            send(block, block, s_x.at[k, 0], r_x.at[k, 0], x_peer, c),
            send(block, block, s_x.at[k, 1], r_x.at[k, 1], core_peer, c),
        ]

    def x_forward(k):
        xs[k][0].wait_recv()
        block = batch.at[k, x_peer]
        xs[k].append(send(block, block, s_x.at[k, 2], r_x.at[k, 2], core_peer, c))

    def x_done(k):
        xs[k][1].wait_recv()
        xs[k][2].wait_recv()

    rs, cg, lg = {}, {}, {}

    def ar_start(k):
        rs[k] = [
            send(part.at[k, p], rs_in.at[k, L], s_rs.at[k, d], r_rs.at[k, d], p, c)
            for d, p in enumerate(lpeer)
        ]
        rs_in[k, L] = part[k, L]

    def ar_mid(k):
        for copy in rs[k]:
            copy.wait_recv()
        cg_in[k, c] = sum((rs_in[k, p] for p in range(1, nl)), rs_in[k, 0])
        cg[k] = [
            send(cg_in.at[k, c], cg_in.at[k, c], s_cg.at[k, d], r_cg.at[k, d], L, p)
            for d, p in enumerate(cpeer)
        ]

    def ar_fin(k):
        for copy in cg[k]:
            copy.wait_recv()
        quarter[k, L] = sum((cg_in[k, p] for p in range(1, nc)), cg_in[k, 0])
        lg[k] = [
            send(quarter.at[k, L], quarter.at[k, L], s_lg.at[k, d], r_lg.at[k, d], p, c)
            for d, p in enumerate(lpeer)
        ]

    def residual(k):
        for copy in lg[k]:
            copy.wait_recv()
        for p in range(nl):
            lo = k * chunk + p * qw
            pred_ref[:, lo:lo + qw] = quarter[k, p]
            diff = quarter[k, p] - targets_ref[:, lo:lo + qw]
            resid[:, lo:lo + qw] = -2.0 * diff.astype(BF16)

    scale = -4.0 / math.sqrt(cen.shape[1])

    def prepare(k):
        one = jnp.ones((8, cen.shape[1]), BF16)
        rows = batch[k].reshape(chunk, cen.shape[1])
        for s in range(n_sub):
            r = rows[s * SUB:(s + 1) * SUB].astype(F32)
            rows2[s] = jnp.transpose((-2.0 * r).astype(BF16))
            sq = r * r
            hi = sq.astype(BF16)
            lo = (sq - hi.astype(F32)).astype(BF16)
            row_sq[s] = dot(one, hi, NT) + dot(one, lo, NT)
            z = jnp.maximum(dot(nys_cen, rows2[s]) + row_sq[s, 0:1, :] + nys_sq, 1e-30)
            nys_kern[k * n_sub + s] = jnp.exp((z * lax.rsqrt(z)) * scale).astype(BF16)

    def cross(s, t, buf):
        at = pl.ds(pl.multiple_of(t * CT, CT), CT)
        buf[...] = dot(cen[at, :], rows2[s])

    def values(k, s, t, buf):
        row = jnp.broadcast_to(row_sq[s, 0:1, :], (STRIP, SUB))
        for i in range(CT // STRIP):
            at = pl.ds(pl.multiple_of(t * CT + i * STRIP, STRIP), STRIP)
            side = jnp.concatenate([cen_b[at, :]] * (SUB // 128), axis=1)
            z = jnp.maximum(buf[i * STRIP:(i + 1) * STRIP, :] + row + side, 1e-30)
            kern[k * n_sub + s, at, :] = jnp.exp((z * lax.rsqrt(z)) * scale).astype(BF16)

    def weigh(k, s, t):
        at = pl.ds(pl.multiple_of(t * CT, CT), CT)
        return dot(w_half[:, at], kern[k * n_sub + s, at, :])

    tiles = n_cen // CT

    def compute(k, between):
        for s in range(n_sub):
            def step(u, acc):
                t = 2 * u
                before = weigh(k, s, jnp.maximum(t - 1, 0))
                acc = acc + jnp.where(u > 0, before, 0.0)
                cross(s, t + 1, buf_b)
                values(k, s, t, buf_a)
                cross(s, jnp.minimum(t + 2, tiles - 1), buf_a)
                acc = acc + weigh(k, s, t)
                values(k, s, t + 1, buf_b)
                return acc

            cross(s, 0, buf_a)
            acc = lax.fori_loop(0, tiles // 4, step, jnp.zeros((16, SUB), F32))
            if s == 0:
                between()
            acc = lax.fori_loop(tiles // 4, tiles // 2, step, acc)
            acc = acc + weigh(k, s, tiles - 1)
            width = min(qw, SUB)
            for q in range(SUB // width):
                lo = s * SUB + q * width
                part[k, lo // qw, :, lo % qw:lo % qw + width] = acc[:, q * width:(q + 1) * width]

    gt = n_cen // GT

    def gradient(k, first=0, end=gt):
        for s in range(n_sub):
            lo = k * chunk + s * SUB

            def step(t, carry):
                at = pl.ds(pl.multiple_of(t * GT, GT), GT)
                term = dot(resid[:, lo:lo + SUB], kern[k * n_sub + s, at, :], NT)
                if lo == 0:
                    grad[:, at] = w[:, at] + term
                else:
                    grad[:, at] = grad[:, at] + term
                return carry

            lax.fori_loop(first, end, step, 0, unroll=2)

    x_send(0)
    x_forward(0)
    x_done(0)
    if nch > 1:
        x_send(1)
    for k in range(nch):
        prepare(k)

        def between():
            if k + 1 < nch:
                x_forward(k + 1)
            if k >= 1:
                ar_mid(k - 1)

        compute(k, between)
        if k + 1 < nch:
            x_done(k + 1)
        if k + 2 < nch:
            x_send(k + 2)
        ar_start(k)
        if k >= 1:
            ar_fin(k - 1)
    last = nch - 1
    for k in range(min(1, last)):
        residual(k)
        gradient(k)
    ar_mid(last)
    for k in range(1, min(2, last)):
        residual(k)
        gradient(k)
    ar_fin(last)
    for k in range(2, last):
        residual(k)
        gradient(k)
    residual(last)
    nys_grad = jnp.zeros((16, n_nys), F32)
    for q in range(nch * n_sub):
        nys_grad = nys_grad + dot(resid[:, q * SUB:(q + 1) * SUB], nys_kern[q], NT)
    co_own[0] = lax.dot_general(
        nys_grad, eig_ref[...], NN, precision=lax.Precision.HIGHEST, preferred_element_type=F32
    )
    c1 = [
        send(co_own.at[0], co_in.at[L], s_c1.at[d], r_c1.at[d], p, c)
        for d, p in enumerate(lpeer)
    ]
    co_in[L] = co_own[0]
    gradient(last, 0, gt // 2)
    for copy in c1:
        copy.wait_recv()
    co_own[1] = sum((co_in[p] for p in range(1, nl)), co_in[0])
    c2 = [
        send(co_own.at[1], co_in2.at[c], s_c2.at[d], r_c2.at[d], L, p)
        for d, p in enumerate(cpeer)
    ]
    co_in2[c] = co_own[1]
    gradient(last, gt // 2, gt)
    for copy in c2:
        copy.wait_recv()
    coeff_ref[...] = sum((co_in2[p] for p in range(1, nc)), co_in2[0]) * damp_ref[...]

    for copy in started:
        copy.wait_send()


def finish(nys_ref, eig_ref, coeff_ref, grad_ref, pred_ref, out_ref, pred_out):
    pred_out[...] = pred_ref[...]
    lane = lax.broadcasted_iota(jnp.int32, (16, 128), 1)
    delta = lax.dot_general(
        coeff_ref[...], eig_ref[...], NT, precision=lax.Precision.HIGHEST, preferred_element_type=F32
    )
    for j in range(eig_ref.shape[0]):
        lo = j * 128
        hit = lane == nys_ref[j] - lo
        out_ref[:, lo:lo + 128] = grad_ref[:, lo:lo + 128] - jnp.where(hit, delta[:, j:j + 1], 0.0)


def body(pool, batch_index, targets, centers, weights, nys_index, eigvecs, damping):
    nl, nc = lax.axis_size("loader"), lax.axis_size("centers")
    rows = batch_index.shape[0]
    nch = rows // (nl * nc * PIECE)
    chunk = rows // nch
    width = centers.shape[1]
    n_cen = centers.shape[0]
    n_nys = nys_index.shape[0]
    qw = nc * PIECE
    index = batch_index.reshape(nch * nl, nc * PIECE)
    dma = lambda *s: [pltpu.SemaphoreType.DMA(s), pltpu.SemaphoreType.DMA(s)]
    vmem = pl.BlockSpec(memory_space=pltpu.VMEM)
    hbm = pl.BlockSpec(memory_space=pl.ANY)
    smem = pl.BlockSpec(memory_space=pltpu.SMEM)
    grad, pred, coeff = pl.pallas_call(
        functools.partial(kernel, nl, nc, nch),
        out_shape=(
            jax.ShapeDtypeStruct(weights.shape, F32),
            jax.ShapeDtypeStruct(targets.shape, F32),
            jax.ShapeDtypeStruct((16, eigvecs.shape[1]), F32),
        ),
        in_specs=[vmem, smem, vmem, vmem, vmem, hbm, hbm, hbm],
        out_specs=(vmem, vmem, vmem),
        scratch_shapes=[
            pltpu.VMEM(pool.shape, BF16),
            pltpu.VMEM(centers.shape, BF16),
            pltpu.VMEM(weights.shape, F32),
            pltpu.VMEM(weights.shape, BF16),
            pltpu.VMEM((rows // SUB, n_cen, SUB), BF16),
            pltpu.VMEM((n_cen, 128), F32),
            pltpu.VMEM((chunk // SUB, width, SUB), BF16),
            pltpu.VMEM((chunk // SUB, 8, SUB), F32),
            pltpu.VMEM((nch, nl, qw, width), BF16),
            pltpu.VMEM((nl, nch * PIECE, width), BF16),
            pltpu.VMEM((nl, nch * PIECE, width), BF16),
            pltpu.VMEM((nch, PIECE, width), BF16),
            pltpu.VMEM((nch, nl, 16, qw), F32),
            pltpu.VMEM((nch, nl, 16, qw), F32),
            pltpu.VMEM((nch, nc, 16, qw), F32),
            pltpu.VMEM((nch, nl, 16, qw), F32),
            pltpu.VMEM((16, rows), BF16),
            pltpu.VMEM((n_nys, width), F32),
            pltpu.VMEM((rows // SUB, n_nys, SUB), BF16),
            pltpu.VMEM((nl, 16, 128), F32),
            pltpu.VMEM((nc, 16, 128), F32),
            pltpu.VMEM((2, 16, 128), F32),
            pltpu.VMEM((CT, SUB), F32),
            pltpu.VMEM((CT, SUB), F32),
            pltpu.SemaphoreType.DMA((3,)),
            *dma(nl - 1), *dma(nch, nc - 1), *dma(nch, 3), *dma(nch, nl - 1),
            *dma(nch, nc - 1), *dma(nch, nl - 1), *dma(nl - 1), *dma(nc - 1),
        ],
        compiler_params=pltpu.CompilerParams(
            collective_id=0, has_side_effects=True, vmem_limit_bytes=62 * 1024 * 1024
        ),
    )(index, nys_index, targets, eigvecs, damping.reshape(1, -1), pool, centers, weights)
    return pl.pallas_call(
        finish,
        out_shape=(
            jax.ShapeDtypeStruct(weights.shape, F32),
            jax.ShapeDtypeStruct(targets.shape, F32),
        ),
        in_specs=[smem, vmem, vmem, vmem, vmem],
        out_specs=(vmem, vmem),
    )(nys_index, eigvecs, coeff, grad, pred)


def solution(mesh):
    return jax.shard_map(
        body,
        mesh=mesh,
        in_specs=(
            P("loader", None),
            P(),
            P(),
            P(("loader", "centers"), None),
            P(None, ("loader", "centers")),
            P(("loader", "centers")),
            P(("loader", "centers"), None),
            P(),
        ),
        out_specs=(P(None, ("loader", "centers")), P()),
        check_vma=False,
    )
```
